256 devices in a mesh: dp: 8 (over z), expert: 32 (over y, x, core).
Axes of the slice: x: 4, y: 4, z: 8, core: 2. Of those that a mesh axis runs over, the one named last changes fastest.
Arguments:
- activations: bfloat16 [32768, 4096], P(('dp', 'expert')), may hold values from -6 to 6
- out_grads: bfloat16 [32768, 2, 4096], P(('dp', 'expert')), may hold values from -6 to 6
- routes: int32 [32768, 2], P(('dp', 'expert')), may hold values from 0 to 7, as said below
Outputs:
- act_factor: float32 [32, 512, 4096], P('expert', 'dp')
- grad_factor: float32 [32, 512, 4096], P('expert', 'dp')
The draws below stay inside these ranges and needn't reach their ends.
Inputs may be any that keep to these rules, and one draw needn't show every extreme that they name: `routes`: each row names 2 different experts. Among the 128 rows of one device no expert is named more than 48 times. One expert below 4, the same on every device, is named exactly 48 times by every device's rows, and on some device every expert below 4 is named exactly 48 times.
All inputs are finite; a program needn't handle non-finite values.
Results may differ from the reference program's by a relative error of at most 0.0003.
Values may be sent and summed in bfloat16 or wider, within the bound.
No kernel may reach another device: no remote copies, remote signals or barrier semaphores. Data moves between devices by JAX's collectives and lax.ppermute only.
A program may use at most 128 MiB of HBM per device.

```python
import jax
import jax.numpy as jnp
from jax import lax

D = 4096
EXPERTS = 8
TOP = 2
EXP_WIN = 4
TOK_DEV = 128
CAP = 48
SPLIT = 8
PIECE = 512
TOKENS = 32768


def draw_routes(key, part):
    key = jax.random.fold_in(key, 11)
    key_hot, key_star, key_dev = jax.random.split(key, 3)
    blocks = TOKENS // TOK_DEV
    slot_total = EXPERTS * CAP
    hot = jax.random.randint(key_hot, (), 0, EXP_WIN).astype(jnp.int32)
    star = jax.random.randint(key_star, (), 0, blocks).astype(jnp.int32)
    expert_ids = jnp.arange(EXPERTS, dtype=jnp.int32)
    slot_expert = jnp.arange(slot_total, dtype=jnp.int32) // CAP
    positions = jnp.arange(TOP * TOK_DEV, dtype=jnp.int32)

    def one_device(dev_key, index):
        key_full, key_other, key_slot, key_tok, key_flip = jax.random.split(dev_key, 5)
        full_count = jax.random.randint(key_full, (), 1, 6).astype(jnp.int32)
        others = (hot + 1 + jax.random.permutation(key_other, EXPERTS - 1).astype(jnp.int32)) % EXPERTS
        rank_of = jnp.zeros((EXPERTS,), jnp.int32).at[others].set(jnp.arange(1, EXPERTS, dtype=jnp.int32))
        special = index == star
        full = jnp.where(special, expert_ids < EXP_WIN, rank_of < full_count)
        full_num = jnp.sum(full.astype(jnp.int32))
        remain = TOP * TOK_DEV - CAP * full_num
        slot_full = full[slot_expert].astype(jnp.int32)
        scores = slot_full * slot_total + jax.random.permutation(key_slot, slot_total).astype(jnp.int32)
        order = jnp.argsort(scores, stable=True).astype(jnp.int32)
        picked = (jnp.arange(slot_total, dtype=jnp.int32) < remain).astype(jnp.int32)
        chosen = jnp.zeros((slot_total,), jnp.int32).at[order].set(picked)
        counts = CAP * full.astype(jnp.int32) + chosen.reshape(EXPERTS, CAP).sum(axis=1)
        ends = jnp.cumsum(counts)
        sequence = jnp.sum((positions[:, None] >= ends[None, :]).astype(jnp.int32), axis=1)
        pairs = jnp.stack([sequence[:TOK_DEV], sequence[TOK_DEV:]], axis=-1)
        flip = jax.random.randint(key_flip, (TOK_DEV, 1), 0, 2)
        pairs = jnp.where(flip == 1, pairs[:, ::-1], pairs)
        return pairs[jax.random.permutation(key_tok, TOK_DEV)]
    routes = jax.vmap(one_device)(jax.random.split(key_dev, blocks), jnp.arange(blocks, dtype=jnp.int32))
    return routes.reshape(TOKENS, TOP).astype(jnp.int32)


def level_of(own_key, extent, cuts, least, high):
    loudness, own = 1.0, jax.random.fold_in(own_key, 6)
    for dim, shards_of in cuts:
        steps = jnp.exp(jax.random.uniform(jax.random.fold_in(own, dim), (shards_of,), jnp.float32, least / len(cuts), high / len(cuts)))
        loudness = loudness * jnp.repeat(steps, extent[dim] // shards_of).reshape([-1 if axis == dim else 1 for axis in range(len(extent))])
    return loudness


def bell_draw(stream_key, shape, width, bound, cuts=(), held_as=jnp.bfloat16):
    array = jax.random.normal(stream_key, shape, jnp.float32) * width
    if len(cuts) > 0:
        array = level_of(stream_key, shape, cuts, -0.22, 0.18) * array
    return jnp.clip(array, min=-bound, max=bound).astype(held_as)


def setup_inputs(seed: int = 0) -> dict:
    streams_of = jax.random.split(jax.random.key(seed), 4)
    return {
        "activations": bell_draw(streams_of[0], (TOKENS, D), 1.0, 6.0, ((0, 256),)),
        "out_grads": bell_draw(streams_of[1], (TOKENS, TOP, D), 1.0, 6.0, ((0, 256),)),
        "routes": draw_routes(jax.random.fold_in(streams_of[3], 71), 0),
    }


def reference(activations, out_grads, routes):
    flat_routes = routes.reshape(TOKENS * TOP)
    flat_grads = out_grads.reshape(TOKENS * TOP, D)
    kept = (TOKENS // TOK_DEV) * CAP
    scale_norm = TOKENS * TOP / EXPERTS

    def single(expert):
        hit = (flat_routes == expert).astype(jnp.int32)
        order = jnp.argsort(1 - hit, stable=True)[:kept].astype(jnp.int32)
        weight = hit[order].astype(jnp.float32)[:, None]
        rows_act = activations[order // TOP].astype(jnp.float32) * weight
        rows_grad = flat_grads[order].astype(jnp.float32) * weight
        act_full = jnp.dot(rows_act.T, rows_act, precision=lax.Precision.HIGHEST)
        grad_full = jnp.dot(rows_grad.T, rows_grad, precision=lax.Precision.HIGHEST)
        return act_full / scale_norm, grad_full / scale_norm

    act_all, grad_all = lax.map(single, jnp.arange(EXP_WIN, dtype=jnp.int32))
    return act_all.reshape(EXP_WIN * SPLIT, PIECE, D), grad_all.reshape(EXP_WIN * SPLIT, PIECE, D)
```

```python
import jax
import jax.numpy as jnp
from jax import lax
from jax.experimental import pallas as pl
from jax.experimental.pallas import tpu as pltpu
from jax.sharding import Mesh, PartitionSpec as P

EXPERTS = 8
TOP = 2
EXP_WIN = 4
CAP = 48
TILE = 512


def shift(size, step):
    return [(i, (i + step) % size) for i in range(size)]


def gram_kernel(strip_ref, *refs):
    blocks = (len(refs) - 3) // 2
    left_refs, right_refs = refs[:blocks], refs[blocks : 2 * blocks]
    out_ref, left, right = refs[2 * blocks :]
    rows = left_refs[0].shape[0]

    @pl.when(pl.program_id(0) == 0)
    def _():
        for i, ref in enumerate(left_refs):
            left[i * rows : (i + 1) * rows, :] = ref[...]

    for i, ref in enumerate(right_refs):
        right[i * rows : (i + 1) * rows, :] = ref[...]
    out_ref[...] = lax.dot_general(
        left[...], right[...], (((0,), (0,)), ((), ())), preferred_element_type=jnp.float32
    ) * jnp.float32(1.0 / SCALE)


SCALE = 8192.0


def gram(strip, blocks, piece):
    rows, width = blocks[0].shape
    count = len(blocks)
    flops = 2 * count * rows * piece * width
    return pl.pallas_call(
        gram_kernel,
        out_shape=jax.ShapeDtypeStruct((piece, width), jnp.float32),
        grid_spec=pltpu.PrefetchScalarGridSpec(
            num_scalar_prefetch=1,
            grid=(width // TILE,),
            in_specs=[pl.BlockSpec((rows, piece), lambda j, s: (0, s[0]))] * count
            + [pl.BlockSpec((rows, TILE), lambda j, s: (0, j))] * count,
            out_specs=pl.BlockSpec((piece, TILE), lambda j, s: (0, j)),
            scratch_shapes=[
                pltpu.VMEM((count * rows, piece), jnp.bfloat16),
                pltpu.VMEM((count * rows, TILE), jnp.bfloat16),
            ],
        ),
        compiler_params=pltpu.CompilerParams(vmem_limit_bytes=40 * 2**20),
        cost_estimate=pl.CostEstimate(
            flops=flops, bytes_accessed=count * rows * width * 2 + piece * width * 4, transcendentals=0
        ),
    )(strip, *blocks, *blocks)


def ring_sum(part, groups):
    z = lax.axis_index("z")
    rows = part.shape[0] // groups
    half = rows // 2
    up, down = shift(groups, 1), shift(groups, -1)

    def chunk(step, first, count):
        at = lax.rem(z + step + groups, groups) * rows + first
        return lax.dynamic_slice_in_dim(part, at, count, 0)

    far = groups // 2
    from_low = lax.ppermute(chunk(far, 0, half), "z", up)
    from_high = lax.ppermute(chunk(-far, half, half), "z", down)
    for step in range(far - 1, 0, -1):
        own_up, own_down = chunk(step, 0, rows), chunk(-step, 0, rows)
        if step == far - 1:
            own_up = jnp.concatenate([own_up[:half] + from_low, own_up[half:]], axis=0)
            own_down = jnp.concatenate([own_down[:half], own_down[half:] + from_high], axis=0)
        else:
            own_up, own_down = own_up + from_low, own_down + from_high
        from_low = lax.ppermute(own_up, "z", up)
        from_high = lax.ppermute(own_down, "z", down)
    return chunk(0, 0, rows) + (from_low + from_high)


def spread(send):
    width = send.shape[-1]
    mine = lax.all_to_all(send, "y", split_axis=0, concat_axis=0, tiled=True)
    mine = mine.reshape(-1, width)
    chips = lax.axis_size("x")
    held = [mine] + [lax.ppermute(mine, "x", shift(chips, step)) for step in (1, chips - 1, 2)]
    return held + [lax.ppermute(block, "c", shift(2, 1)) for block in held]


def on_device(activations, out_grads, routes):
    tok_rows = activations.shape[0]
    width = activations.shape[1]
    groups = lax.axis_size("z")
    split = lax.axis_size("x") * lax.axis_size("c")
    piece = width // split
    flat_routes = routes.reshape(TOP * tok_rows)
    hits = (flat_routes[:, None] == jnp.arange(EXP_WIN, dtype=jnp.int32)[None, :]).astype(jnp.int32)
    slots = jnp.cumsum(hits, axis=0) - hits
    placed = hits[:, :, None] * (
        slots[:, :, None] == jnp.arange(CAP, dtype=jnp.int32)[None, None, :]
    ).astype(jnp.int32)
    placed = (
        jnp.transpose(placed, (1, 2, 0)).reshape(EXP_WIN * CAP, TOP * tok_rows).astype(jnp.bfloat16)
    )
    token_placed = placed.reshape(EXP_WIN * CAP, tok_rows, TOP).sum(axis=-1)
    send_act = jnp.dot(token_placed, activations, preferred_element_type=jnp.float32).astype(
        jnp.bfloat16
    )
    send_grad = jnp.dot(
        placed, out_grads.reshape(TOP * tok_rows, width), preferred_element_type=jnp.float32
    ).astype(jnp.bfloat16)
    strip = (lax.axis_index("x") * 2 + lax.axis_index("c")).astype(jnp.int32).reshape(1)
    act_rows = spread(send_act.reshape(EXP_WIN, CAP, width))
    act_part = gram(strip, act_rows, piece)
    act_block = lax.psum_scatter(act_part, "z", scatter_dimension=0, tiled=True)
    grad_rows = spread(send_grad.reshape(EXP_WIN, CAP, width))
    grad_part = gram(strip, grad_rows, piece)
    grad_block = ring_sum(grad_part, groups)
    return act_block[None], grad_block[None]


def solution(mesh):
    axes = ("z", "y", "x", "c")
    fine = Mesh(mesh.devices.reshape(8, 4, 4, 2), axes)
    placed = (P(axes, None), P(axes, None, None), P(axes, None))
    return jax.shard_map(
        on_device,
        mesh=fine,
        in_specs=placed,
        out_specs=(P(("y", "x", "c"), "z", None), P(("y", "x", "c"), "z", None)),
        check_vma=False,
    )
```

```python
import jax
import jax.numpy as jnp
from jax import lax
from jax.experimental import pallas as pl
from jax.experimental.pallas import tpu as pltpu
from jax.sharding import Mesh, PartitionSpec as P

EXPERTS = 8
TOP = 2
EXP_WIN = 4
CAP = 48
TILE = 512
LANES = 128
ROWS = 16
FINE = 128.0
LEVELS = 32767.0


def shift(size, step):
    return [(i, (i + step) % size) for i in range(size)]


def gram_kernel(strip_ref, *refs):
    blocks = (len(refs) - 3) // 2
    left_refs, right_refs = refs[:blocks], refs[blocks : 2 * blocks]
    out_ref, left, right = refs[2 * blocks :]

    def stack(into, parts):
        at = 0
        for part in parts:
            into[at : at + part.shape[0], :] = part[...]
            at += part.shape[0]

    @pl.when(pl.program_id(0) == 0)
    def _():
        stack(left, left_refs)

    stack(right, right_refs)
    out_ref[...] = lax.dot_general(
        left[...], right[...], (((0,), (0,)), ((), ())), preferred_element_type=jnp.float32
    )


def gram(strip, blocks, piece):
    width = blocks[0].shape[1]
    rows = sum(block.shape[0] for block in blocks)
    return pl.pallas_call(
        gram_kernel,
        out_shape=jax.ShapeDtypeStruct((piece, width), jnp.float32),
        grid_spec=pltpu.PrefetchScalarGridSpec(
            num_scalar_prefetch=1,
            grid=(width // TILE,),
            in_specs=[pl.BlockSpec((b.shape[0], piece), lambda j, s: (0, s[0])) for b in blocks]
            + [pl.BlockSpec((b.shape[0], TILE), lambda j, s: (0, j)) for b in blocks],
            out_specs=pl.BlockSpec((piece, TILE), lambda j, s: (0, j)),
            scratch_shapes=[
                pltpu.VMEM((rows, piece), jnp.bfloat16),
                pltpu.VMEM((rows, TILE), jnp.bfloat16),
            ],
        ),
        compiler_params=pltpu.CompilerParams(vmem_limit_bytes=40 * 2**20),
        cost_estimate=pl.CostEstimate(
            flops=2 * rows * piece * width,
            bytes_accessed=rows * width * 2 + piece * width * 4,
            transcendentals=0,
        ),
    )(strip, *blocks, *blocks)


def encode(values, out_ref):
    rows, width = values.shape
    lane = lax.broadcasted_iota(jnp.int32, (rows, LANES), 1)
    top = jnp.zeros((rows, LANES), jnp.float32)
    for b in range(width // LANES):
        most = jnp.max(jnp.abs(values[:, b * LANES : (b + 1) * LANES]), axis=1, keepdims=True)
        top = jnp.where(lane == b, most, top)
    code = jnp.ceil(jnp.log2(jnp.maximum(top, 2.0**-126)) * FINE)
    shrink = jnp.exp2(code * (-1.0 / FINE))
    out_ref[:, width:] = code.astype(jnp.int32).astype(jnp.int16)
    for b in range(width // LANES):
        cut = slice(b * LANES, (b + 1) * LANES)
        level = jnp.round(values[:, cut] * shrink[:, b : b + 1] * LEVELS)
        level = jnp.clip(level, -LEVELS, LEVELS)
        out_ref[:, cut] = level.astype(jnp.int32).astype(jnp.int16)


def add_decoded(total, coded_ref):
    rows, width = total.shape
    code = coded_ref[:, width:].astype(jnp.int32).astype(jnp.float32)
    unit = jnp.exp2(code * (1.0 / FINE)) * (1.0 / LEVELS)
    for b in range(width // LANES):
        cut = slice(b * LANES, (b + 1) * LANES)
        total[:, cut] += coded_ref[:, cut].astype(jnp.int32).astype(jnp.float32) * unit[:, b : b + 1]


def first_kernel(at_ref, up_own, down_own, up_out, down_out):
    encode(up_own, up_out)
    encode(down_own, down_out)


def step_kernel(at_ref, up_own, down_own, up_in, down_in, up_out, down_out, total):
    halved = at_ref[2] == 1
    i = pl.program_id(0)
    half = pl.num_programs(0) // 2
    for own, got, out, here in (
        (up_own, up_in, up_out, jnp.logical_or(jnp.logical_not(halved), i < half)),
        (down_own, down_in, down_out, jnp.logical_or(jnp.logical_not(halved), i >= half)),
    ):
        total[...] = own[...]

        @pl.when(here)
        def _():
            add_decoded(total, got)

        encode(total, out)


def last_kernel(at_ref, scale_ref, own, up_in, down_in, out_ref):
    out_ref[...] = own[...]
    add_decoded(out_ref, up_in)
    add_decoded(out_ref, down_in)
    out_ref[...] = out_ref[...] * scale_ref[0]


def ring_sum(part, groups, scale):
    z = lax.axis_index("z").astype(jnp.int32)
    width = part.shape[1]
    rows = part.shape[0] // groups
    bands = rows // ROWS
    far = groups // 2
    up, down = shift(groups, 1), shift(groups, -1)

    def place(step):
        return lax.rem(z + step + groups, groups) * bands

    def own(k):
        return pl.BlockSpec((ROWS, width), lambda i, at: (at[k] + i, 0))

    def coded(fn):
        return pl.BlockSpec((ROWS, width + LANES), lambda i, at: (fn(i), 0))

    def call(kernel, at, bands, ins, in_specs, scratch=()):
        return pl.pallas_call(
            kernel,
            out_shape=[jax.ShapeDtypeStruct((bands * ROWS, width + LANES), jnp.int16)] * 2,
            grid_spec=pltpu.PrefetchScalarGridSpec(
                num_scalar_prefetch=1,
                grid=(bands,),
                in_specs=in_specs,
                out_specs=[coded(lambda i: i)] * 2,
                scratch_shapes=list(scratch),
            ),
            cost_estimate=pl.CostEstimate(
                flops=16 * bands * ROWS * width,
                bytes_accessed=16 * bands * ROWS * width,
                transcendentals=0,
            ),
        )(at, *ins)

    sends = call(
        first_kernel,
        jnp.stack([place(far), place(far) + bands // 2]),
        bands // 2,
        (part, part),
        [own(0), own(1)],
    )
    for step in range(far - 1, 0, -1):
        got = lax.ppermute(sends[0], "z", up), lax.ppermute(sends[1], "z", down)
        halved = step == far - 1
        half = bands // 2
        specs = (
            [coded(lambda i: jnp.minimum(i, half - 1)), coded(lambda i: jnp.maximum(i - half, 0))]
            if halved
            else [coded(lambda i: i)] * 2
        )
        sends = call(
            step_kernel,
            jnp.stack([place(step), place(-step), jnp.int32(halved)]),
            bands,
            (part, part) + got,
            [own(0), own(1)] + specs,
            [pltpu.VMEM((ROWS, width), jnp.float32)],
        )
    got = lax.ppermute(sends[0], "z", up), lax.ppermute(sends[1], "z", down)
    return pl.pallas_call(
        last_kernel,
        out_shape=jax.ShapeDtypeStruct((rows, width), jnp.float32),
        grid_spec=pltpu.PrefetchScalarGridSpec(
            num_scalar_prefetch=2,
            grid=(bands,),
            in_specs=[
                pl.BlockSpec((ROWS, width), lambda i, at, s: (at[0] + i, 0)),
                pl.BlockSpec((ROWS, width + LANES), lambda i, at, s: (i, 0)),
                pl.BlockSpec((ROWS, width + LANES), lambda i, at, s: (i, 0)),
            ],
            out_specs=pl.BlockSpec((ROWS, width), lambda i, at, s: (i, 0)),
        ),
        cost_estimate=pl.CostEstimate(
            flops=16 * rows * width, bytes_accessed=12 * rows * width, transcendentals=0
        ),
    )(place(0).reshape(1), jnp.full((1,), scale, jnp.float32), part, *got)


def exchange(sends, axis):
    chips = lax.axis_size(axis)
    order = (1, chips - 1, 2)
    return [sends[0]] + [lax.ppermute(sends[d], axis, shift(chips, d)) for d in order]


def gather(blocks, axis):
    chips = lax.axis_size(axis)
    up, down = shift(chips, 1), shift(chips, -1)
    half = len(blocks) // 2
    low = jnp.concatenate(blocks[:half], axis=0)
    high = jnp.concatenate(blocks[half:], axis=0)
    low_up = lax.ppermute(low, axis, up)
    high_down = lax.ppermute(high, axis, down)
    high_up = lax.ppermute(high, axis, up)
    low_down = lax.ppermute(low, axis, down)
    low_far = lax.ppermute(low_up, axis, up)
    high_far = lax.ppermute(high_down, axis, down)
    held = [low, high, low_up, high_down, high_up, low_down, low_far, high_far]
    return held + [lax.ppermute(block, "c", shift(2, 1)) for block in held]


def on_device(activations, out_grads, routes):
    tok_rows = activations.shape[0]
    width = activations.shape[1]
    groups = lax.axis_size("z")
    chips = lax.axis_size("x")
    split = chips * lax.axis_size("c")
    piece = width // split
    scale_norm = tok_rows * groups * EXP_WIN * split * TOP / EXPERTS
    x, y, core = (lax.axis_index(axis).astype(jnp.int32) for axis in ("x", "y", "c"))
    flat_grads = out_grads.reshape(TOP * tok_rows, width)
    flat_routes = routes.reshape(TOP * tok_rows)

    def placing(first):
        experts = lax.rem(first + jnp.arange(EXP_WIN, dtype=jnp.int32), EXP_WIN)
        hits = (flat_routes[None, :] == experts[:, None]).astype(jnp.int32)
        slots = jnp.cumsum(hits, axis=1) - hits
        slot = jnp.arange(CAP, dtype=jnp.int32)
        chosen = (slots[:, None, :] == slot[None, :, None]) & (hits[:, None, :] == 1)
        return chosen.reshape(EXP_WIN * CAP, TOP * tok_rows)

    def pack(rows, data):
        sent = jnp.dot(rows.astype(jnp.bfloat16), data, preferred_element_type=jnp.float32)
        return sent.astype(jnp.bfloat16).reshape(EXP_WIN, CAP, width)

    act_rows = placing(y).reshape(EXP_WIN * CAP, tok_rows, TOP).any(axis=-1)
    send_act = pack(act_rows, activations)
    send_grad = pack(placing(x), flat_grads)

    act = jnp.concatenate(exchange(send_act, "y"), axis=0)
    grad = exchange(send_grad, "x")
    act = lax.all_gather(act, ("x", "c"), tiled=True)
    grad = gather(grad, "y")
    grad_strip = lax.rem(x + y, chips) * 2 + core
    grad_part = gram(grad_strip.reshape(1), grad, piece)
    act_part = gram((x * 2 + core).reshape(1), [act], piece)
    grad_block = ring_sum(grad_part, groups, 1.0 / scale_norm)
    act_block = ring_sum(act_part, groups, 1.0 / scale_norm)
    moves = [
        (b * chips + a, a * chips + (a + b) % chips) for b in range(chips) for a in range(chips)
    ]
    grad_block = lax.ppermute(grad_block, ("y", "x"), moves)
    return act_block[None], grad_block[None]


def solution(mesh):
    axes = ("z", "y", "x", "c")
    fine = Mesh(mesh.devices.reshape(8, 4, 4, 2), axes)
    placed = (P(axes, None), P(axes, None, None), P(axes, None))
    return jax.shard_map(
        on_device,
        mesh=fine,
        in_specs=placed,
        out_specs=(P(("y", "x", "c"), "z", None), P(("y", "x", "c"), "z", None)),
        check_vma=False,
    )
```

```python
import functools

import jax
import jax.numpy as jnp
from jax import lax
from jax.experimental import pallas as pl
from jax.experimental.pallas import tpu as pltpu
from jax.sharding import Mesh, PartitionSpec as P

EXPERTS = 8
TOP = 2
EXP_WIN = 4
CAP = 48
TILE = 1024
LANES = 128
ROWS = 16
FINE = 128.0
LEVELS = 32760.0


def shift(size, step):
    return [(i, (i + step) % size) for i in range(size)]


def gram_kernel(strip_ref, *refs, blocks, based):
    left_refs, right_refs = refs[:blocks], refs[blocks : 2 * blocks]
    out_ref, left, right = refs[-3:]

    def stack(parts):
        at = 0
        for part in parts:
            right[at : at + part.shape[0], : part.shape[1]] = part[...]
            at += part.shape[0]

    @pl.when(pl.program_id(0) == 0)
    def _():
        stack(left_refs)
        left[...] = right[:, : left.shape[0]].T

    stack(right_refs)
    total = jnp.dot(left[...], right[...], preferred_element_type=jnp.float32)
    out_ref[...] = total + refs[2 * blocks][...] if based else total


def gram(strip, blocks, piece, base=None):
    width = blocks[0].shape[1]
    rows = sum(block.shape[0] for block in blocks)
    tile = pl.BlockSpec((piece, TILE), lambda j, s: (0, j))
    extra = () if base is None else (base,)
    return pl.pallas_call(
        functools.partial(gram_kernel, blocks=len(blocks), based=base is not None),
        out_shape=jax.ShapeDtypeStruct((piece, width), jnp.float32),
        grid_spec=pltpu.PrefetchScalarGridSpec(
            num_scalar_prefetch=1,
            grid=(width // TILE,),
            in_specs=[pl.BlockSpec((b.shape[0], piece), lambda j, s: (0, s[0])) for b in blocks]
            + [pl.BlockSpec((b.shape[0], TILE), lambda j, s: (0, j)) for b in blocks]
            + [tile] * len(extra),
            out_specs=tile,
            scratch_shapes=[
                pltpu.VMEM((piece, rows), jnp.bfloat16),
                pltpu.VMEM((rows, TILE), jnp.bfloat16),
            ],
        ),
        input_output_aliases={1 + 2 * len(blocks): 0} if extra else {},
        compiler_params=pltpu.CompilerParams(vmem_limit_bytes=28 * 2**20),
        cost_estimate=pl.CostEstimate(
            flops=4 * rows * piece * width,
            bytes_accessed=rows * width * 2 + piece * width * 4,
            transcendentals=0,
        ),
    )(strip, *blocks, *blocks, *extra)


def encode(values, out_ref):
    width = values.shape[1]
    cuts = [slice(at, at + LANES) for at in range(0, width, LANES)]
    most = jnp.abs(values[:, cuts[0]])
    for cut in cuts[1:]:
        most = jnp.maximum(most, jnp.abs(values[:, cut]))
    code = jnp.ceil(jnp.log2(jnp.maximum(most, 2.0**-126)) * FINE)
    out_ref[:, width:] = code.astype(jnp.int32).astype(jnp.int16)
    shrink = jnp.exp2(code * (-1.0 / FINE))
    for cut in cuts:
        level = jnp.round(values[:, cut] * shrink * LEVELS)
        out_ref[:, cut] = level.astype(jnp.int32).astype(jnp.int16)


def add_decoded(total, coded_ref):
    width = total.shape[1]
    code = coded_ref[:, width:].astype(jnp.int32).astype(jnp.float32)
    unit = jnp.exp2(code * (1.0 / FINE)) * (1.0 / LEVELS)
    for at in range(0, width, LANES):
        cut = slice(at, at + LANES)
        total[:, cut] += coded_ref[:, cut].astype(jnp.int32).astype(jnp.float32) * unit


def first_kernel(at_ref, up_own, down_own, up_out, down_out):
    encode(up_own, up_out)
    encode(down_own, down_out)


def step_kernel(at_ref, up_own, down_own, up_in, down_in, up_out, down_out, total):
    halved = at_ref[2] == 1
    i = pl.program_id(0)
    half = pl.num_programs(0) // 2
    for own, got, out, here in (
        (up_own, up_in, up_out, jnp.logical_or(jnp.logical_not(halved), i < half)),
        (down_own, down_in, down_out, jnp.logical_or(jnp.logical_not(halved), i >= half)),
    ):
        total[...] = own[...]

        @pl.when(here)
        def _():
            add_decoded(total, got)

        encode(total, out)


def last_kernel(at_ref, scale_ref, own, up_in, down_in, out_ref):
    out_ref[...] = own[...]
    add_decoded(out_ref, up_in)
    add_decoded(out_ref, down_in)
    out_ref[...] = out_ref[...] * scale_ref[0]


def ring_calls(part, groups):
    z = lax.axis_index("z").astype(jnp.int32)
    width = part.shape[1]
    rows = part.shape[0] // groups
    bands = rows // ROWS
    half = bands // 2
    far = groups // 2
    params = pltpu.CompilerParams(vmem_limit_bytes=8 * 2**20)

    def place(step):
        return lax.rem(z + step + groups, groups) * bands

    def own(k):
        return pl.BlockSpec((ROWS, width), lambda i, at: (at[k] + i, 0))

    def coded(fn=lambda i: i):
        return pl.BlockSpec((ROWS, width + LANES), lambda i, at: (fn(i), 0))

    def call(kernel, at, bands, ins, in_specs, scratch=()):
        return pl.pallas_call(
            kernel,
            out_shape=[jax.ShapeDtypeStruct((bands * ROWS, width + LANES), jnp.int16)] * 2,
            grid_spec=pltpu.PrefetchScalarGridSpec(
                num_scalar_prefetch=1,
                grid=(bands,),
                in_specs=in_specs,
                out_specs=[coded()] * 2,
                scratch_shapes=list(scratch),
            ),
            compiler_params=params,
            cost_estimate=pl.CostEstimate(
                flops=16 * bands * ROWS * width,
                bytes_accessed=12 * bands * ROWS * width,
                transcendentals=0,
            ),
        )(at, *ins)

    def first():
        at = jnp.stack([place(far), place(far) + half])
        return call(first_kernel, at, half, (part, part), [own(0), own(1)])

    def middle(step, got):
        halved = step == far - 1
        specs = (
            [coded(lambda i: jnp.minimum(i, half - 1)), coded(lambda i: jnp.maximum(i - half, 0))]
            if halved
            else [coded()] * 2
        )
        at = jnp.stack([place(step), place(-step), jnp.int32(halved)])
        scratch = [pltpu.VMEM((ROWS, width), jnp.float32)]
        return call(step_kernel, at, bands, (part, part) + got, [own(0), own(1)] + specs, scratch)

    def last(got, scale):
        return pl.pallas_call(
            last_kernel,
            out_shape=jax.ShapeDtypeStruct((rows, width), jnp.float32),
            grid_spec=pltpu.PrefetchScalarGridSpec(
                num_scalar_prefetch=2,
                grid=(bands,),
                in_specs=[
                    pl.BlockSpec((ROWS, width), lambda i, at, s: (at[0] + i, 0)),
                    pl.BlockSpec((ROWS, width + LANES), lambda i, at, s: (i, 0)),
                    pl.BlockSpec((ROWS, width + LANES), lambda i, at, s: (i, 0)),
                ],
                out_specs=pl.BlockSpec((ROWS, width), lambda i, at, s: (i, 0)),
            ),
            compiler_params=params,
            cost_estimate=pl.CostEstimate(
                flops=16 * rows * width, bytes_accessed=12 * rows * width, transcendentals=0
            ),
        )(place(0).reshape(1), jnp.full((1,), scale, jnp.float32), part, *got)

    return first, middle, last


def ring_pass(sends, groups):
    return (
        lax.ppermute(sends[0], "z", shift(groups, 1)),
        lax.ppermute(sends[1], "z", shift(groups, -1)),
    )


def after(values, *others):
    return lax.optimization_barrier((values, others))[0]


def exchange(sends, axis):
    chips = lax.axis_size(axis)
    got = [lax.ppermute(sends[d], axis, shift(chips, d)) for d in (1, chips - 1, 2)]
    return jnp.concatenate([sends[0]] + got, axis=0)


def gather(mine, axis):
    chips = lax.axis_size(axis)
    half = mine.shape[0] // 2
    swap = shift(2, 1)
    low = lax.ppermute(mine, axis, shift(chips, 1))
    high = lax.ppermute(mine, axis, shift(chips, -1))
    far_low = lax.ppermute(low[:half], axis, shift(chips, 1))
    far_high = lax.ppermute(high[half:], axis, shift(chips, -1))
    near = [mine, low, high]
    far = [far_low, far_high]
    near += [lax.ppermute(block, "c", swap) for block in near]
    far += [lax.ppermute(block, "c", swap) for block in far]
    return near, far


def on_device(activations, out_grads, routes):
    tok_rows = activations.shape[0]
    width = activations.shape[1]
    groups = lax.axis_size("z")
    chips = lax.axis_size("x")
    split = chips * lax.axis_size("c")
    piece = width // split
    scale = 1.0 / (tok_rows * groups * EXP_WIN * split * TOP / EXPERTS)
    x, y, core = (lax.axis_index(axis).astype(jnp.int32) for axis in ("x", "y", "c"))

    def pack(first, named, data):
        count = data.shape[0]
        experts = lax.rem(first + jnp.arange(EXP_WIN, dtype=jnp.int32), EXP_WIN)
        hits = (named[None] == experts[:, None, None]).any(axis=1)
        ahead = jnp.arange(count)[:, None] < jnp.arange(count)[None, :]
        slots = jnp.dot(
            hits.astype(jnp.bfloat16), ahead.astype(jnp.bfloat16), preferred_element_type=jnp.float32
        ).astype(jnp.int32)
        slot = jnp.arange(CAP, dtype=jnp.int32)
        chosen = (slots[:, None, :] == slot[None, :, None]) & hits[:, None, :]
        chosen = chosen.reshape(EXP_WIN * CAP, count).astype(jnp.bfloat16)
        sent = jnp.dot(chosen, data, preferred_element_type=jnp.float32)
        sent = sent.astype(jnp.bfloat16)
        return [sent[d * CAP : (d + 1) * CAP] for d in range(EXP_WIN)]

    send_act = pack(y, routes.T, activations)
    send_grad = pack(
        x, routes.reshape(1, TOP * tok_rows), out_grads.reshape(TOP * tok_rows, width)
    )
    send_act, send_grad = lax.optimization_barrier((send_act, send_grad))
    grad = exchange(send_grad, "x")
    act = exchange(send_act, "y")
    grad_near, grad_far = gather(grad, "y")
    act_near, act_far = gather(act, "x")
    grad_strip = (lax.rem(x + y, chips) * 2 + core).reshape(1)
    act_strip = (x * 2 + core).reshape(1)
    grad_part = gram(grad_strip, grad_near, piece)
    act_part = gram(act_strip, act_near, piece)
    grad_part = gram(grad_strip, grad_far, piece, grad_part)
    act_part = gram(act_strip, act_far, piece, act_part)

    grad_first, grad_middle, grad_last = ring_calls(grad_part, groups)
    act_first, act_middle, act_last = ring_calls(act_part, groups)
    grad_sends = grad_first()
    grad_got = ring_pass(grad_sends, groups)
    act_sends = act_first()
    act_got = ring_pass(act_sends, groups)
    for step in range(groups // 2 - 1, 0, -1):
        grad_sends = grad_middle(step, after(grad_got, act_sends))
        grad_got = ring_pass(grad_sends, groups)
        act_sends = act_middle(step, after(act_got, grad_sends))
        act_got = ring_pass(act_sends, groups)
    grad_block = grad_last(after(grad_got, act_sends), scale)
    moves = [
        (b * chips + a, a * chips + (a + b) % chips) for b in range(chips) for a in range(chips)
    ]
    grad_block = lax.ppermute(grad_block, ("y", "x"), moves)
    act_block = act_last(act_got, scale)
    return act_block[None], grad_block[None]


def solution(mesh):
    axes = ("z", "y", "x", "c")
    fine = Mesh(mesh.devices.reshape(8, 4, 4, 2), axes)
    placed = (P(axes, None), P(axes, None, None), P(axes, None))
    return jax.shard_map(
        on_device,
        mesh=fine,
        in_specs=placed,
        out_specs=(P(("y", "x", "c"), "z", None), P(("y", "x", "c"), "z", None)),
        check_vma=False,
    )
```

```python
import functools

import jax
import jax.numpy as jnp
from jax import lax
from jax.experimental import pallas as pl
from jax.experimental.pallas import tpu as pltpu
from jax.sharding import Mesh, PartitionSpec as P

EXPERTS = 8
TOP = 2
EXP_WIN = 4
CAP = 48
TILE = 1024
LANES = 128
ROWS = 32
FINE = 128.0
LEVELS = 32760.0


def shift(size, step):
    return [(i, (i + step) % size) for i in range(size)]


def gram_kernel(at_ref, *refs, blocks, order, groups):
    count = len(order)
    left_refs, right_refs = refs[:blocks], refs[blocks : 2 * blocks]
    base_refs, out_refs = refs[2 * blocks : -3 - count], refs[-3 - count : -3]
    turned, left, right = refs[-3:]
    size = turned.shape[0] // groups

    def stack(parts):
        at = 0
        for part in parts:
            right[at : at + part.shape[0], : part.shape[1]] = part[...]
            at += part.shape[0]

    @pl.when(pl.program_id(0) == 0)
    def _():
        stack(left_refs)
        turned[...] = right[:, : turned.shape[0]].T
        for i, k in enumerate(order):
            first = pl.multiple_of(lax.rem(at_ref[1] + k, groups) * size, size)
            left[i * size : (i + 1) * size, :] = turned[pl.ds(first, size), :]

    stack(right_refs)
    total = jnp.dot(left[...], right[...], preferred_element_type=jnp.float32)
    for i, out_ref in enumerate(out_refs):
        rows = total[i * size : (i + 1) * size]
        out_ref[...] = rows + base_refs[i][...] if base_refs else rows


def gram(at, blocks, piece, groups, order, bases=(), wide=TILE):
    width = blocks[0].shape[1]
    rows = sum(block.shape[0] for block in blocks)
    blocks = [pltpu.with_memory_space_constraint(block, pltpu.HBM) for block in blocks]
    size = piece // groups
    tile = pl.BlockSpec((size, wide), lambda j, s: (0, j))
    return pl.pallas_call(
        functools.partial(gram_kernel, blocks=len(blocks), order=order, groups=groups),
        out_shape=[jax.ShapeDtypeStruct((size, width), jnp.float32)] * len(order),
        grid_spec=pltpu.PrefetchScalarGridSpec(
            num_scalar_prefetch=1,
            grid=(width // wide,),
            in_specs=[pl.BlockSpec((b.shape[0], piece), lambda j, s: (0, s[0])) for b in blocks]
            + [pl.BlockSpec((b.shape[0], wide), lambda j, s: (0, j)) for b in blocks]
            + [tile] * len(bases),
            out_specs=[tile] * len(order),
            scratch_shapes=[
                pltpu.VMEM((piece, rows), jnp.bfloat16),
                pltpu.VMEM((len(order) * size, rows), jnp.bfloat16),
                pltpu.VMEM((rows, wide), jnp.bfloat16),
            ],
        ),
        compiler_params=pltpu.CompilerParams(vmem_limit_bytes=20 * 2**20),
        cost_estimate=pl.CostEstimate(
            flops=(0 if len(order) == groups else 4) * rows * piece * width,
            bytes_accessed=rows * width,
            transcendentals=0,
        ),
    )(at, *blocks, *blocks, *bases)


def encode(values, out_ref):
    width = values.shape[1]
    cuts = [slice(at, at + LANES) for at in range(0, width, LANES)]
    most = jnp.abs(values[:, cuts[0]])
    for cut in cuts[1:]:
        most = jnp.maximum(most, jnp.abs(values[:, cut]))
    code = jnp.ceil(jnp.log2(jnp.maximum(most, 2.0**-126)) * FINE)
    out_ref[:, width:] = code.astype(jnp.int32).astype(jnp.int16)
    shrink = jnp.exp2(code * (-1.0 / FINE))
    for cut in cuts:
        level = jnp.round(values[:, cut] * shrink * LEVELS)
        out_ref[:, cut] = level.astype(jnp.int32).astype(jnp.int16)


def add_decoded(total, coded_ref):
    width = total.shape[1]
    code = coded_ref[:, width:].astype(jnp.int32).astype(jnp.float32)
    unit = jnp.exp2(code * (1.0 / FINE)) * (1.0 / LEVELS)
    for at in range(0, width, LANES):
        cut = slice(at, at + LANES)
        total[:, cut] += coded_ref[:, cut].astype(jnp.int32).astype(jnp.float32) * unit


def first_kernel(up_own, down_own, up_out, down_out):
    encode(up_own, up_out)
    encode(down_own, down_out)


def step_kernel(up_own, down_own, up_in, down_in, up_out, down_out, total, *, halved):
    i = pl.program_id(0)
    half = pl.num_programs(0) // 2
    for own, got, out, here in (
        (up_own, up_in, up_out, i < half),
        (down_own, down_in, down_out, i >= half),
    ):
        total[...] = own[...]
        if halved:
            pl.when(here)(functools.partial(add_decoded, total, got))
        else:
            add_decoded(total, got)
        encode(total, out)


def last_kernel(own, up_in, down_in, out_ref, total, *, scale):
    total[...] = own[...]
    add_decoded(total, up_in)
    add_decoded(total, down_in)
    if scale is None:
        encode(total, out_ref)
    else:
        out_ref[...] = total[...] * jnp.float32(scale)


def unpack_kernel(coded, out_ref, *, scale):
    out_ref[...] = jnp.zeros_like(out_ref)
    add_decoded(out_ref, coded)
    out_ref[...] = out_ref[...] * jnp.float32(scale)


def unpack(coded, scale):
    rows, width = coded.shape[0], coded.shape[1] - LANES
    return pl.pallas_call(
        functools.partial(unpack_kernel, scale=scale),
        out_shape=jax.ShapeDtypeStruct((rows, width), jnp.float32),
        grid=(rows // ROWS,),
        in_specs=[pl.BlockSpec((ROWS, width + LANES), lambda i: (i, 0))],
        out_specs=pl.BlockSpec((ROWS, width), lambda i: (i, 0)),
        compiler_params=pltpu.CompilerParams(vmem_limit_bytes=8 * 2**20),
    )(coded)


def ring_calls(parts, groups):
    rows, width = next(iter(parts.values())).shape
    bands = rows // ROWS
    half = bands // 2
    far = groups // 2

    def own(fn=lambda i: i):
        return pl.BlockSpec((ROWS, width), lambda i: (fn(i), 0))

    def coded(fn=lambda i: i):
        return pl.BlockSpec((ROWS, width + LANES), lambda i: (fn(i), 0))

    def call(kernel, bands, ins, in_specs, out=None, out_spec=None, scratch=()):
        if out is None:
            out = [jax.ShapeDtypeStruct((bands * ROWS, width + LANES), jnp.int16)] * 2
        return pl.pallas_call(
            kernel,
            out_shape=out,
            grid=(bands,),
            in_specs=in_specs,
            out_specs=[coded()] * 2 if isinstance(out, list) else out_spec,
            scratch_shapes=list(scratch),
            compiler_params=pltpu.CompilerParams(vmem_limit_bytes=8 * 2**20),
            cost_estimate=pl.CostEstimate(
                flops=10**10, bytes_accessed=40 * rows * width, transcendentals=0
            ),
        )(*ins)

    def first():
        part = parts[far]
        return call(first_kernel, half, (part, part), [own(), own(lambda i: half + i)])

    def middle(step, got):
        halved = step == far - 1
        specs = (
            [coded(lambda i: jnp.minimum(i, half - 1)), coded(lambda i: jnp.maximum(i - half, 0))]
            if halved
            else [coded()] * 2
        )
        return call(
            functools.partial(step_kernel, halved=halved),
            bands,
            (parts[step], parts[groups - step]) + got,
            [own(), own()] + specs,
            scratch=[pltpu.VMEM((ROWS, width), jnp.float32)],
        )

    def last(got, scale):
        if scale is None:
            out, spec = jax.ShapeDtypeStruct((rows, width + LANES), jnp.int16), coded()
        else:
            out, spec = jax.ShapeDtypeStruct((rows, width), jnp.float32), own()
        return call(
            functools.partial(last_kernel, scale=scale),
            bands,
            (parts[0],) + got,
            [own(), coded(), coded()],
            out,
            spec,
            [pltpu.VMEM((ROWS, width), jnp.float32)],
        )

    return first, middle, last


def ring_pass(sends, groups):
    return (
        lax.ppermute(sends[0], "z", shift(groups, 1)),
        lax.ppermute(sends[1], "z", shift(groups, -1)),
    )


def after(values, *others):
    return lax.optimization_barrier((values, others))[0]


def exchange(sends, axis):
    chips = lax.axis_size(axis)
    got = [lax.ppermute(sends[d], axis, shift(chips, d)) for d in (2, 1, chips - 1)]
    return jnp.concatenate([sends[0]] + got, axis=0)


def neighbours(mine, axis):
    chips = lax.axis_size(axis)
    return [lax.ppermute(mine, axis, shift(chips, step)) for step in (1, chips - 1)]


def opposite(near, axis):
    chips = lax.axis_size(axis)
    half = near[0].shape[0] // 2
    low = lax.ppermute(near[0][:half], axis, shift(chips, 1))
    high = lax.ppermute(near[1][half:], axis, shift(chips, -1))
    return [low, high]


def both_cores(blocks):
    return blocks + [lax.ppermute(block, "c", shift(2, 1)) for block in blocks]


def on_device(activations, out_grads, routes):
    tok_rows = activations.shape[0]
    width = activations.shape[1]
    groups = lax.axis_size("z")
    chips = lax.axis_size("x")
    split = chips * lax.axis_size("c")
    piece = width // split
    scale = 1.0 / (tok_rows * groups * EXP_WIN * split * TOP / EXPERTS)
    z, y, x, core = (lax.axis_index(axis).astype(jnp.int32) for axis in ("z", "y", "x", "c"))

    def pack(first, named, data):
        count = data.shape[0]
        experts = lax.rem(first + jnp.arange(EXP_WIN, dtype=jnp.int32), EXP_WIN)
        hits = (named[None] == experts[:, None, None]).any(axis=1)
        ahead = jnp.arange(count)[:, None] < jnp.arange(count)[None, :]
        slots = jnp.dot(
            hits.astype(jnp.bfloat16), ahead.astype(jnp.bfloat16), preferred_element_type=jnp.float32
        ).astype(jnp.int32)
        slot = jnp.arange(CAP, dtype=jnp.int32)
        chosen = (slots[:, None, :] == slot[None, :, None]) & hits[:, None, :]
        chosen = chosen.reshape(EXP_WIN * CAP, count).astype(jnp.bfloat16)
        sent = jnp.dot(chosen, data, preferred_element_type=jnp.float32)
        sent = sent.astype(jnp.bfloat16)
        return [sent[d * CAP : (d + 1) * CAP] for d in range(EXP_WIN)]

    send_act = pack(y, routes.T, activations)
    send_grad = pack(
        x, routes.reshape(1, TOP * tok_rows), out_grads.reshape(TOP * tok_rows, width)
    )
    send_act, send_grad = lax.optimization_barrier((send_act, send_grad))
    grad = exchange(send_grad, "x")
    act = exchange(send_act, "y")
    far = groups // 2
    order = [far] + [k for step in range(far - 1, 0, -1) for k in (step, groups - step)] + [0]
    grad_at = jnp.stack([lax.rem(x + y, chips) * 2 + core, z])
    act_at = jnp.stack([x * 2 + core, z])
    grad_near, act_near = neighbours(grad, "y"), neighbours(act, "x")
    grad_part = gram(grad_at, both_cores([grad]), piece, groups, order)
    act_part = gram(act_at, both_cores([act]), piece, groups, order)
    grad_near, act_near = after((grad_near, act_near), grad_part, act_part)
    grad_far, act_far = opposite(grad_near, "y"), opposite(act_near, "x")
    grad_part = gram(grad_at, both_cores(grad_near), piece, groups, order, grad_part)
    act_part = gram(act_at, both_cores(act_near), piece, groups, order, act_part)
    grad_far, act_far = after((grad_far, act_far), grad_part, act_part)
    grad_far, act_far = both_cores(grad_far), both_cores(act_far)
    grad_parts = gram(grad_at, grad_far, piece, groups, order[:3], grad_part[:3], 2 * TILE)
    act_parts = gram(act_at, act_far, piece, groups, order[:3], act_part[:3], 2 * TILE)

    grad_first, grad_middle, grad_last = ring_calls(dict(zip(order, grad_parts)), groups)
    act_first, act_middle, act_last = ring_calls(dict(zip(order, act_parts)), groups)
    grad_sends = grad_first()
    grad_got = ring_pass(grad_sends, groups)
    act_sends = act_first()
    act_got = ring_pass(act_sends, groups)
    for step in range(far - 1, 0, -1):
        grad_sends = grad_middle(step, after(grad_got, act_sends))
        grad_got = ring_pass(grad_sends, groups)
        act_sends = act_middle(step, after(act_got, grad_sends))
        act_got = ring_pass(act_sends, groups)
        if step == far - 1:
            rest, bases = order[3:], after((grad_part[3:], act_part[3:]), grad_sends, act_sends)
            grad_parts = gram(grad_at, grad_far, piece, groups, rest, bases[0], 2 * TILE)
            act_parts = gram(act_at, act_far, piece, groups, rest, bases[1], 2 * TILE)
            _, grad_middle, grad_last = ring_calls(dict(zip(rest, grad_parts)), groups)
            _, act_middle, act_last = ring_calls(dict(zip(rest, act_parts)), groups)
    moves = [
        (b * chips + a, a * chips + (a + b) % chips) for b in range(chips) for a in range(chips)
    ]
    grad_block = grad_last(after(grad_got, act_sends), None)
    grad_block = unpack(lax.ppermute(grad_block, ("y", "x"), moves), scale)
    act_block = act_last(act_got, scale)
    return act_block[None], grad_block[None]


def solution(mesh):
    axes = ("z", "y", "x", "c")
    fine = Mesh(mesh.devices.reshape(8, 4, 4, 2), axes)
    placed = (P(axes, None), P(axes, None, None), P(axes, None))
    return jax.shard_map(
        on_device,
        mesh=fine,
        in_specs=placed,
        out_specs=(P(("y", "x", "c"), "z", None), P(("y", "x", "c"), "z", None)),
        check_vma=False,
    )
```

```python
import functools

import jax
import jax.numpy as jnp
from jax import lax
from jax.experimental import pallas as pl
from jax.experimental.pallas import tpu as pltpu
from jax.sharding import Mesh, PartitionSpec as P

EXPERTS = 8
TOP = 2
EXP_WIN = 4
CAP = 48
TILE = 1024
LANES = 128
ROWS = 32
FINE = 128.0
LEVELS = 32760.0


def shift(size, step):
    return [(i, (i + step) % size) for i in range(size)]


def gram_kernel(at_ref, *refs, blocks, order, groups):
    count = len(order)
    left_refs, right_refs = refs[:blocks], refs[blocks : 2 * blocks]
    base_refs, out_refs = refs[2 * blocks : -3 - count], refs[-3 - count : -3]
    turned, left, right = refs[-3:]
    size = turned.shape[0] // groups

    def stack(parts):
        at = 0
        for part in parts:
            right[at : at + part.shape[0], : part.shape[1]] = part[...]
            at += part.shape[0]

    @pl.when(pl.program_id(0) == 0)
    def _():
        stack(left_refs)
        turned[...] = right[:, : turned.shape[0]].T
        for i, k in enumerate(order):
            first = pl.multiple_of(lax.rem(at_ref[1] + k, groups) * size, size)
            left[i * size : (i + 1) * size, :] = turned[pl.ds(first, size), :]

    stack(right_refs)
    total = jnp.dot(left[...], right[...], preferred_element_type=jnp.float32)
    for i, out_ref in enumerate(out_refs):
        rows = total[i * size : (i + 1) * size]
        out_ref[...] = rows + base_refs[i][...] if base_refs else rows


def gram(at, blocks, piece, groups, order, bases=(), wide=TILE):
    width = blocks[0].shape[1]
    rows = sum(block.shape[0] for block in blocks)
    if sum(block.shape[0] for block in blocks) > 384:
        blocks = [pltpu.with_memory_space_constraint(block, pltpu.HBM) for block in blocks]
    size = piece // groups
    tile = pl.BlockSpec((size, wide), lambda j, s: (0, j))
    return pl.pallas_call(
        functools.partial(gram_kernel, blocks=len(blocks), order=order, groups=groups),
        out_shape=[jax.ShapeDtypeStruct((size, width), jnp.float32)] * len(order),
        grid_spec=pltpu.PrefetchScalarGridSpec(
            num_scalar_prefetch=1,
            grid=(width // wide,),
            in_specs=[pl.BlockSpec((b.shape[0], piece), lambda j, s: (0, s[0])) for b in blocks]
            + [pl.BlockSpec((b.shape[0], wide), lambda j, s: (0, j)) for b in blocks]
            + [tile] * len(bases),
            out_specs=[tile] * len(order),
            scratch_shapes=[
                pltpu.VMEM((piece, rows), jnp.bfloat16),
                pltpu.VMEM((len(order) * size, rows), jnp.bfloat16),
                pltpu.VMEM((rows, wide), jnp.bfloat16),
            ],
        ),
        compiler_params=pltpu.CompilerParams(vmem_limit_bytes=16 * 2**20),
        cost_estimate=pl.CostEstimate(
            flops=(4 if wide > TILE else 0) * rows * piece * width,
            bytes_accessed=rows * width,
            transcendentals=0,
        ),
    )(at, *blocks, *blocks, *bases)


def encode(values, out_ref):
    width = values.shape[1]
    cuts = [slice(at, at + LANES) for at in range(0, width, LANES)]
    most = jnp.abs(values[:, cuts[0]])
    for cut in cuts[1:]:
        most = jnp.maximum(most, jnp.abs(values[:, cut]))
    code = jnp.ceil(jnp.log2(jnp.maximum(most, 2.0**-126)) * FINE)
    out_ref[:, width:] = code.astype(jnp.int32).astype(jnp.int16)
    shrink = jnp.exp2(code * (-1.0 / FINE))
    for cut in cuts:
        level = jnp.round(values[:, cut] * shrink * LEVELS)
        out_ref[:, cut] = level.astype(jnp.int32).astype(jnp.int16)


def add_decoded(total, coded_ref):
    width = total.shape[1]
    code = coded_ref[:, width:].astype(jnp.int32).astype(jnp.float32)
    unit = jnp.exp2(code * (1.0 / FINE)) * (1.0 / LEVELS)
    for at in range(0, width, LANES):
        cut = slice(at, at + LANES)
        total[:, cut] += coded_ref[:, cut].astype(jnp.int32).astype(jnp.float32) * unit


def first_kernel(up_own, down_own, up_out, down_out):
    encode(up_own, up_out)
    encode(down_own, down_out)


def step_kernel(up_own, down_own, up_in, down_in, up_out, down_out, total, *, halved):
    i = pl.program_id(0)
    half = pl.num_programs(0) // 2
    for own, got, out, here in (
        (up_own, up_in, up_out, i < half),
        (down_own, down_in, down_out, i >= half),
    ):
        total[...] = own[...]
        if halved:
            pl.when(here)(functools.partial(add_decoded, total, got))
        else:
            add_decoded(total, got)
        encode(total, out)


def last_kernel(own, up_in, down_in, out_ref, total, *, scale):
    total[...] = own[...]
    add_decoded(total, up_in)
    add_decoded(total, down_in)
    if scale is None:
        encode(total, out_ref)
    else:
        out_ref[...] = total[...] * jnp.float32(scale)


def unpack_kernel(coded, out_ref, *, scale):
    out_ref[...] = jnp.zeros_like(out_ref)
    add_decoded(out_ref, coded)
    out_ref[...] = out_ref[...] * jnp.float32(scale)


def unpack(coded, scale):
    rows, width = coded.shape[0], coded.shape[1] - LANES
    return pl.pallas_call(
        functools.partial(unpack_kernel, scale=scale),
        out_shape=jax.ShapeDtypeStruct((rows, width), jnp.float32),
        grid=(rows // ROWS,),
        in_specs=[pl.BlockSpec((ROWS, width + LANES), lambda i: (i, 0))],
        out_specs=pl.BlockSpec((ROWS, width), lambda i: (i, 0)),
        compiler_params=pltpu.CompilerParams(vmem_limit_bytes=8 * 2**20),
    )(coded)


def ring_calls(parts, groups):
    rows, width = next(iter(parts.values())).shape
    bands = rows // ROWS
    half = bands // 2
    far = groups // 2

    def own(fn=lambda i: i):
        return pl.BlockSpec((ROWS, width), lambda i: (fn(i), 0))

    def coded(fn=lambda i: i):
        return pl.BlockSpec((ROWS, width + LANES), lambda i: (fn(i), 0))

    def call(kernel, bands, ins, in_specs, out=None, out_spec=None, scratch=()):
        if out is None:
            out = [jax.ShapeDtypeStruct((bands * ROWS, width + LANES), jnp.int16)] * 2
        return pl.pallas_call(
            kernel,
            out_shape=out,
            grid=(bands,),
            in_specs=in_specs,
            out_specs=[coded()] * 2 if isinstance(out, list) else out_spec,
            scratch_shapes=list(scratch),
            compiler_params=pltpu.CompilerParams(vmem_limit_bytes=8 * 2**20),
            cost_estimate=pl.CostEstimate(
                flops=10**10, bytes_accessed=40 * rows * width, transcendentals=0
            ),
        )(*ins)

    def first():
        part = parts[far]
        return call(first_kernel, half, (part, part), [own(), own(lambda i: half + i)])

    def middle(step, got):
        halved = step == far - 1
        specs = (
            [coded(lambda i: jnp.minimum(i, half - 1)), coded(lambda i: jnp.maximum(i - half, 0))]
            if halved
            else [coded()] * 2
        )
        return call(
            functools.partial(step_kernel, halved=halved),
            bands,
            (parts[step], parts[groups - step]) + got,
            [own(), own()] + specs,
            scratch=[pltpu.VMEM((ROWS, width), jnp.float32)],
        )

    def last(got, scale):
        if scale is None:
            out, spec = jax.ShapeDtypeStruct((rows, width + LANES), jnp.int16), coded()
        else:
            out, spec = jax.ShapeDtypeStruct((rows, width), jnp.float32), own()
        return call(
            functools.partial(last_kernel, scale=scale),
            bands,
            (parts[0],) + got,
            [own(), coded(), coded()],
            out,
            spec,
            [pltpu.VMEM((ROWS, width), jnp.float32)],
        )

    return first, middle, last


def ring_pass(sends, groups):
    return (
        lax.ppermute(sends[0], "z", shift(groups, 1)),
        lax.ppermute(sends[1], "z", shift(groups, -1)),
    )


def after(values, *others):
    return lax.optimization_barrier((values, others))[0]


def exchange(sends, axis):
    chips = lax.axis_size(axis)
    got = [lax.ppermute(sends[d], axis, shift(chips, d)) for d in (2, 1, chips - 1)]
    return [sends[0]] + got


def neighbours(mine, axis):
    chips = lax.axis_size(axis)
    return [lax.ppermute(mine, axis, shift(chips, step)) for step in (1, chips - 1)]


def halves_kernel(*refs):
    count = len(refs) // 2
    for ref, out_ref in zip(refs[:count], refs[count:]):
        out_ref[...] = ref[...]


def halves(arrays):
    rows, width = arrays[0].shape[0] // 2, arrays[0].shape[1]
    steps = rows // ROWS
    return pl.pallas_call(
        halves_kernel,
        out_shape=[jax.ShapeDtypeStruct((rows, width), arrays[0].dtype)] * len(arrays),
        grid=(steps,),
        in_specs=[
            pl.BlockSpec((ROWS, width), lambda i, first=k % 2 * steps: (first + i, 0))
            for k in range(len(arrays))
        ],
        out_specs=[pl.BlockSpec((ROWS, width), lambda i: (i, 0))] * len(arrays),
        compiler_params=pltpu.CompilerParams(vmem_limit_bytes=8 * 2**20),
    )(*arrays)


def opposite(pair, axis):
    chips = lax.axis_size(axis)
    return [lax.ppermute(pair[0], axis, shift(chips, 1)), lax.ppermute(pair[1], axis, shift(chips, -1))]


def both_cores(blocks):
    return blocks + [lax.ppermute(block, "c", shift(2, 1)) for block in blocks]


def on_device(activations, out_grads, routes):
    tok_rows = activations.shape[0]
    width = activations.shape[1]
    groups = lax.axis_size("z")
    chips = lax.axis_size("x")
    split = chips * lax.axis_size("c")
    piece = width // split
    scale = 1.0 / (tok_rows * groups * EXP_WIN * split * TOP / EXPERTS)
    z, y, x, core = (lax.axis_index(axis).astype(jnp.int32) for axis in ("z", "y", "x", "c"))

    def pack(first, named, data):
        count = data.shape[0]
        experts = lax.rem(first + jnp.arange(EXP_WIN, dtype=jnp.int32), EXP_WIN)
        hits = (named[None] == experts[:, None, None]).any(axis=1)
        ahead = jnp.arange(count)[:, None] < jnp.arange(count)[None, :]
        slots = jnp.dot(
            hits.astype(jnp.bfloat16), ahead.astype(jnp.bfloat16), preferred_element_type=jnp.float32
        ).astype(jnp.int32)
        slot = jnp.arange(CAP, dtype=jnp.int32)
        chosen = (slots[:, None, :] == slot[None, :, None]) & hits[:, None, :]
        chosen = chosen.reshape(EXP_WIN * CAP, count).astype(jnp.bfloat16)
        sent = jnp.dot(chosen, data, preferred_element_type=jnp.float32)
        sent = sent.astype(jnp.bfloat16)
        return [sent[d * CAP : (d + 1) * CAP] for d in range(EXP_WIN)]

    send_act = pack(y, routes.T, activations)
    send_grad = pack(
        x, routes.reshape(1, TOP * tok_rows), out_grads.reshape(TOP * tok_rows, width)
    )
    send_act, send_grad = lax.optimization_barrier((send_act, send_grad))
    act = jnp.concatenate(exchange(send_act, "y"), axis=0)
    grad = jnp.concatenate(exchange(send_grad, "x"), axis=0)
    far = groups // 2
    order = [far] + [k for step in range(far - 1, 0, -1) for k in (step, groups - step)] + [0]
    grad_strip = lax.rem(2 * x + chips // 2 + chips - y, chips)
    grad_at = jnp.stack([grad_strip * 2 + core, z])
    act_at = jnp.stack([x * 2 + core, z])
    grad_near, act_near = neighbours(grad, "y"), neighbours(act, "x")
    grad_part = gram(grad_at, both_cores([grad]), piece, groups, order)
    act_part = gram(act_at, both_cores([act]), piece, groups, order)
    grad_near, act_near = after(grad_near, grad_part), after(act_near, act_part)
    grad_far, act_far = opposite(halves(grad_near), "y"), opposite(halves(act_near), "x")
    grad_near, act_near = both_cores(grad_near), both_cores(act_near)
    grad_parts = gram(grad_at, grad_near, piece, groups, order[:3], grad_part[:3])
    act_parts = gram(act_at, act_near, piece, groups, order[:3], act_part[:3])
    grad_far, act_far = after(grad_far, grad_parts, act_parts), after(act_far, act_parts)
    grad_far, act_far = both_cores(grad_far), both_cores(act_far)
    grad_parts = gram(grad_at, grad_far, piece, groups, order[:3], grad_parts, 2 * TILE)
    act_parts = gram(act_at, act_far, piece, groups, order[:3], act_parts, 2 * TILE)

    grad_first, grad_middle, grad_last = ring_calls(dict(zip(order, grad_parts)), groups)
    act_first, act_middle, act_last = ring_calls(dict(zip(order, act_parts)), groups)
    grad_sends = grad_first()
    grad_got = ring_pass(grad_sends, groups)
    act_sends = act_first()
    act_got = ring_pass(act_sends, groups)
    for step in range(far - 1, 0, -1):
        grad_sends = grad_middle(step, after(grad_got, act_sends))
        grad_got = ring_pass(grad_sends, groups)
        act_sends = act_middle(step, after(act_got, grad_sends))
        act_got = ring_pass(act_sends, groups)
        rest = {far - 1: order[3:5], far - 2: order[5:]}.get(step)
        if rest:
            at = order.index(rest[0])
            bases = grad_part[at : at + len(rest)], act_part[at : at + len(rest)]
            bases = after(bases, grad_sends, act_sends)
            grad_parts = gram(grad_at, grad_near + grad_far, piece, groups, rest, bases[0])
            act_parts = gram(act_at, act_near + act_far, piece, groups, rest, bases[1])
            _, grad_middle, grad_last = ring_calls(dict(zip(rest, grad_parts)), groups)
            _, act_middle, act_last = ring_calls(dict(zip(rest, act_parts)), groups)
    moves = [
        (b * chips + a, a * chips + (2 * a + chips // 2 - b) % chips)
        for b in range(chips)
        for a in range(chips)
    ]
    grad_block = grad_last(after(grad_got, act_sends), None)
    grad_block = unpack(lax.ppermute(grad_block, ("y", "x"), moves), scale)
    act_block = act_last(act_got, scale)
    return act_block[None], grad_block[None]


def solution(mesh):
    axes = ("z", "y", "x", "c")
    fine = Mesh(mesh.devices.reshape(8, 4, 4, 2), axes)
    placed = (P(axes, None), P(axes, None, None), P(axes, None))
    return jax.shard_map(
        on_device,
        mesh=fine,
        in_specs=placed,
        out_specs=(P(("y", "x", "c"), "z", None), P(("y", "x", "c"), "z", None)),
        check_vma=False,
    )
```

```python
import functools

import jax
import jax.numpy as jnp
from jax import lax
from jax.experimental import pallas as pl
from jax.experimental.pallas import tpu as pltpu
from jax.sharding import Mesh, PartitionSpec as P

EXPERTS = 8
TOP = 2
EXP_WIN = 4
CAP = 48
TILE = 1024
LANES = 128
ROWS = 32
FINE = 128.0
LEVELS = 32760.0


def shift(size, step):
    return [(i, (i + step) % size) for i in range(size)]


def gram_kernel(at_ref, *refs, blocks, order, groups):
    count = len(order)
    left_refs, right_refs = refs[:blocks], refs[blocks : 2 * blocks]
    base_refs, out_refs = refs[2 * blocks : -3 - count], refs[-3 - count : -3]
    turned, left, right = refs[-3:]
    size = turned.shape[0] // groups

    def stack(parts):
        at = 0
        for part in parts:
            right[at : at + part.shape[0], : part.shape[1]] = part[...]
            at += part.shape[0]

    @pl.when(pl.program_id(0) == 0)
    def _():
        stack(left_refs)
        turned[...] = right[:, : turned.shape[0]].T
        for i, k in enumerate(order):
            first = pl.multiple_of(lax.rem(at_ref[1] + k, groups) * size, size)
            left[i * size : (i + 1) * size, :] = turned[pl.ds(first, size), :]

    stack(right_refs)
    total = jnp.dot(left[...], right[...], preferred_element_type=jnp.float32)
    for i, out_ref in enumerate(out_refs):
        rows = total[i * size : (i + 1) * size]
        out_ref[...] = rows + base_refs[i][...] if base_refs else rows


def gram(at, blocks, piece, groups, order, bases=(), wide=TILE):
    width = blocks[0].shape[1]
    rows = sum(block.shape[0] for block in blocks)
    if sum(block.shape[0] for block in blocks) > 384:
        blocks = [pltpu.with_memory_space_constraint(block, pltpu.HBM) for block in blocks]
    size = piece // groups
    tile = pl.BlockSpec((size, wide), lambda j, s: (0, j))
    return pl.pallas_call(
        functools.partial(gram_kernel, blocks=len(blocks), order=order, groups=groups),
        out_shape=[jax.ShapeDtypeStruct((size, width), jnp.float32)] * len(order),
        grid_spec=pltpu.PrefetchScalarGridSpec(
            num_scalar_prefetch=1,
            grid=(width // wide,),
            in_specs=[pl.BlockSpec((b.shape[0], piece), lambda j, s: (0, s[0])) for b in blocks]
            + [pl.BlockSpec((b.shape[0], wide), lambda j, s: (0, j)) for b in blocks]
            + [tile] * len(bases),
            out_specs=[tile] * len(order),
            scratch_shapes=[
                pltpu.VMEM((piece, rows), jnp.bfloat16),
                pltpu.VMEM((len(order) * size, rows), jnp.bfloat16),
                pltpu.VMEM((rows, wide), jnp.bfloat16),
            ],
        ),
        compiler_params=pltpu.CompilerParams(vmem_limit_bytes=16 * 2**20),
        cost_estimate=pl.CostEstimate(
            flops=(4 if wide > TILE else 0) * rows * piece * width,
            bytes_accessed=rows * width,
            transcendentals=0,
        ),
    )(at, *blocks, *blocks, *bases)


def encode(values, out_ref):
    width = values.shape[1]
    cuts = [slice(at, at + LANES) for at in range(0, width, LANES)]
    most = jnp.abs(values[:, cuts[0]])
    for cut in cuts[1:]:
        most = jnp.maximum(most, jnp.abs(values[:, cut]))
    code = jnp.ceil(jnp.log2(jnp.maximum(most, 2.0**-126)) * FINE)
    out_ref[:, width:] = code.astype(jnp.int32).astype(jnp.int16)
    shrink = jnp.exp2(code * (-1.0 / FINE))
    for cut in cuts:
        level = jnp.round(values[:, cut] * shrink * LEVELS)
        out_ref[:, cut] = level.astype(jnp.int32).astype(jnp.int16)


def add_decoded(total, coded_ref):
    width = total.shape[1]
    code = coded_ref[:, width:].astype(jnp.int32).astype(jnp.float32)
    unit = jnp.exp2(code * (1.0 / FINE)) * (1.0 / LEVELS)
    for at in range(0, width, LANES):
        cut = slice(at, at + LANES)
        total[:, cut] += coded_ref[:, cut].astype(jnp.int32).astype(jnp.float32) * unit


def first_kernel(up_own, down_own, up_out, down_out):
    encode(up_own, up_out)
    encode(down_own, down_out)


def step_kernel(up_own, down_own, up_in, down_in, up_out, down_out, total, *, halved):
    i = pl.program_id(0)
    half = pl.num_programs(0) // 2
    for own, got, out, here in (
        (up_own, up_in, up_out, i < half),
        (down_own, down_in, down_out, i >= half),
    ):
        total[...] = own[...]
        if halved:
            pl.when(here)(functools.partial(add_decoded, total, got))
        else:
            add_decoded(total, got)
        encode(total, out)


def last_kernel(own, up_in, down_in, out_ref, total, *, scale):
    total[...] = own[...]
    add_decoded(total, up_in)
    add_decoded(total, down_in)
    if scale is None:
        encode(total, out_ref)
    else:
        out_ref[...] = total[...] * jnp.float32(scale)


def unpack_kernel(coded, out_ref, *, scale):
    out_ref[...] = jnp.zeros_like(out_ref)
    add_decoded(out_ref, coded)
    out_ref[...] = out_ref[...] * jnp.float32(scale)


def unpack(coded, scale):
    rows, width = coded.shape[0], coded.shape[1] - LANES
    return pl.pallas_call(
        functools.partial(unpack_kernel, scale=scale),
        out_shape=jax.ShapeDtypeStruct((rows, width), jnp.float32),
        grid=(rows // ROWS,),
        in_specs=[pl.BlockSpec((ROWS, width + LANES), lambda i: (i, 0))],
        out_specs=pl.BlockSpec((ROWS, width), lambda i: (i, 0)),
        compiler_params=pltpu.CompilerParams(vmem_limit_bytes=8 * 2**20),
    )(coded)


def ring_calls(parts, groups):
    rows, width = next(iter(parts.values())).shape
    bands = rows // ROWS
    half = bands // 2
    far = groups // 2

    def own(fn=lambda i: i):
        return pl.BlockSpec((ROWS, width), lambda i: (fn(i), 0))

    def coded(fn=lambda i: i):
        return pl.BlockSpec((ROWS, width + LANES), lambda i: (fn(i), 0))

    def call(kernel, bands, ins, in_specs, out=None, out_spec=None, scratch=()):
        if out is None:
            out = [jax.ShapeDtypeStruct((bands * ROWS, width + LANES), jnp.int16)] * 2
        return pl.pallas_call(
            kernel,
            out_shape=out,
            grid=(bands,),
            in_specs=in_specs,
            out_specs=[coded()] * 2 if isinstance(out, list) else out_spec,
            scratch_shapes=list(scratch),
            compiler_params=pltpu.CompilerParams(vmem_limit_bytes=8 * 2**20),
            cost_estimate=pl.CostEstimate(
                flops=10**10, bytes_accessed=40 * rows * width, transcendentals=0
            ),
        )(*ins)

    def first():
        part = parts[far]
        return call(first_kernel, half, (part, part), [own(), own(lambda i: half + i)])

    def middle(step, got):
        halved = step == far - 1
        specs = (
            [coded(lambda i: jnp.minimum(i, half - 1)), coded(lambda i: jnp.maximum(i - half, 0))]
            if halved
            else [coded()] * 2
        )
        return call(
            functools.partial(step_kernel, halved=halved),
            bands,
            (parts[step], parts[groups - step]) + got,
            [own(), own()] + specs,
            scratch=[pltpu.VMEM((ROWS, width), jnp.float32)],
        )

    def last(got, scale):
        if scale is None:
            out, spec = jax.ShapeDtypeStruct((rows, width + LANES), jnp.int16), coded()
        else:
            out, spec = jax.ShapeDtypeStruct((rows, width), jnp.float32), own()
        return call(
            functools.partial(last_kernel, scale=scale),
            bands,
            (parts[0],) + got,
            [own(), coded(), coded()],
            out,
            spec,
            [pltpu.VMEM((ROWS, width), jnp.float32)],
        )

    return first, middle, last


def ring_pass(sends, groups):
    return (
        lax.ppermute(sends[0], "z", shift(groups, 1)),
        lax.ppermute(sends[1], "z", shift(groups, -1)),
    )


def after(values, *others):
    return lax.optimization_barrier((values, others))[0]


def exchange(sends, axis):
    chips = lax.axis_size(axis)
    got = [lax.ppermute(sends[d], axis, shift(chips, d)) for d in (2, 1, chips - 1)]
    return [sends[0]] + got


def neighbours(mine, axis):
    chips = lax.axis_size(axis)
    return [lax.ppermute(mine, axis, shift(chips, step)) for step in (1, chips - 1)]


def halves_kernel(*refs):
    count = len(refs) // 2
    for ref, out_ref in zip(refs[:count], refs[count:]):
        out_ref[...] = ref[...]


def halves(arrays):
    rows, width = arrays[0].shape[0] // 2, arrays[0].shape[1]
    steps = rows // ROWS
    return pl.pallas_call(
        halves_kernel,
        out_shape=[jax.ShapeDtypeStruct((rows, width), arrays[0].dtype)] * len(arrays),
        grid=(steps,),
        in_specs=[
            pl.BlockSpec((ROWS, width), lambda i, first=k % 2 * steps: (first + i, 0))
            for k in range(len(arrays))
        ],
        out_specs=[pl.BlockSpec((ROWS, width), lambda i: (i, 0))] * len(arrays),
        compiler_params=pltpu.CompilerParams(vmem_limit_bytes=8 * 2**20),
    )(*arrays)


def opposite(pair, axis):
    chips = lax.axis_size(axis)
    return [lax.ppermute(pair[0], axis, shift(chips, 1)), lax.ppermute(pair[1], axis, shift(chips, -1))]


def both_cores(blocks):
    return blocks + [lax.ppermute(block, "c", shift(2, 1)) for block in blocks]


def on_device(activations, out_grads, routes):
    tok_rows = activations.shape[0]
    width = activations.shape[1]
    groups = lax.axis_size("z")
    chips = lax.axis_size("x")
    split = chips * lax.axis_size("c")
    piece = width // split
    scale = 1.0 / (tok_rows * groups * EXP_WIN * split * TOP / EXPERTS)
    z, y, x, core = (lax.axis_index(axis).astype(jnp.int32) for axis in ("z", "y", "x", "c"))

    def pack(first, named, data):
        count = data.shape[0]
        experts = lax.rem(first + jnp.arange(EXP_WIN, dtype=jnp.int32), EXP_WIN)
        hits = (named[None] == experts[:, None, None]).any(axis=1)
        ahead = jnp.arange(count)[:, None] < jnp.arange(count)[None, :]
        slots = jnp.dot(
            hits.astype(jnp.bfloat16), ahead.astype(jnp.bfloat16), preferred_element_type=jnp.float32
        ).astype(jnp.int32)
        slot = jnp.arange(CAP, dtype=jnp.int32)
        chosen = (slots[:, None, :] == slot[None, :, None]) & hits[:, None, :]
        chosen = chosen.reshape(EXP_WIN * CAP, count).astype(jnp.bfloat16)
        sent = jnp.dot(chosen, data, preferred_element_type=jnp.float32)
        sent = sent.astype(jnp.bfloat16)
        return [sent[d * CAP : (d + 1) * CAP] for d in range(EXP_WIN)]

    send_act = pack(y, routes.T, activations)
    send_grad = pack(
        x, routes.reshape(1, TOP * tok_rows), out_grads.reshape(TOP * tok_rows, width)
    )
    send_act, send_grad = lax.optimization_barrier((send_act, send_grad))
    act = jnp.concatenate(exchange(send_act, "y"), axis=0)
    grad = jnp.concatenate(exchange(send_grad, "x"), axis=0)
    far = groups // 2
    order = [far] + [k for step in range(far - 1, 0, -1) for k in (step, groups - step)] + [0]
    grad_strip = lax.rem(2 * x + chips // 2 + chips - y, chips)
    grad_at = jnp.stack([grad_strip * 2 + core, z])
    act_at = jnp.stack([x * 2 + core, z])
    grad_near, act_near = neighbours(grad, "y"), neighbours(act, "x")
    grad_part = gram(grad_at, both_cores([grad]), piece, groups, order)
    act_part = gram(act_at, both_cores([act]), piece, groups, order)
    grad_near, act_near = after(grad_near, grad_part), after(act_near, act_part)
    grad_far, act_far = opposite(halves(grad_near), "y"), opposite(halves(act_near), "x")
    grad_near, act_near = both_cores(grad_near), both_cores(act_near)
    grad_near, act_near = lax.optimization_barrier((grad_near, act_near))
    grad_parts = gram(grad_at, grad_near, piece, groups, order[:3], grad_part[:3])
    act_parts = gram(act_at, act_near, piece, groups, order[:3], act_part[:3])
    grad_far, act_far = after(grad_far, grad_parts, act_parts), after(act_far, act_parts)
    grad_far, act_far = both_cores(grad_far), both_cores(act_far)
    grad_parts = gram(grad_at, grad_far, piece, groups, order[:3], grad_parts, 2 * TILE)
    act_parts = gram(act_at, act_far, piece, groups, order[:3], act_parts, 2 * TILE)

    grad_first, grad_middle, grad_last = ring_calls(dict(zip(order, grad_parts)), groups)
    act_first, act_middle, act_last = ring_calls(dict(zip(order, act_parts)), groups)
    grad_sends = grad_first()
    grad_got = ring_pass(grad_sends, groups)
    act_sends = act_first()
    act_got = ring_pass(act_sends, groups)
    for step in range(far - 1, 0, -1):
        grad_sends = grad_middle(step, after(grad_got, act_sends))
        grad_got = ring_pass(grad_sends, groups)
        act_sends = act_middle(step, after(act_got, grad_sends))
        act_got = ring_pass(act_sends, groups)
        rest = {far - 1: order[3:5], far - 2: order[5:]}.get(step)
        if rest:
            at = order.index(rest[0])
            bases = grad_part[at : at + len(rest)], act_part[at : at + len(rest)]
            bases = after(bases, grad_sends, act_sends)
            grad_parts = gram(grad_at, grad_near + grad_far, piece, groups, rest, bases[0])
            act_parts = gram(act_at, act_near + act_far, piece, groups, rest, bases[1])
            _, grad_middle, grad_last = ring_calls(dict(zip(rest, grad_parts)), groups)
            _, act_middle, act_last = ring_calls(dict(zip(rest, act_parts)), groups)
    moves = [
        (b * chips + a, a * chips + (2 * a + chips // 2 - b) % chips)
        for b in range(chips)
        for a in range(chips)
    ]
    grad_block = grad_last(after(grad_got, act_sends), None)
    grad_block = unpack(lax.ppermute(grad_block, ("y", "x"), moves), scale)
    act_block = act_last(act_got, scale)
    return act_block[None], grad_block[None]


def solution(mesh):
    axes = ("z", "y", "x", "c")
    fine = Mesh(mesh.devices.reshape(8, 4, 4, 2), axes)
    placed = (P(axes, None), P(axes, None, None), P(axes, None))
    return jax.shard_map(
        on_device,
        mesh=fine,
        in_specs=placed,
        out_specs=(P(("y", "x", "c"), "z", None), P(("y", "x", "c"), "z", None)),
        check_vma=False,
    )
```
